32 devices in a mesh: layer: 8 (over y, x, core), lat: 4 (over z).
Axes of the slice: x: 2, y: 2, z: 4, core: 2. Of those that a mesh axis runs over, the one named last changes fastest.
Arguments:
- saved_codes: bfloat16 [8, 512, 1024], P('layer', 'lat'), may hold values from 0.049804688 to 2
- relu_mask: int32 [8, 512, 1024], P('layer', 'lat'), may hold values 0 or 1
- errors: bfloat16 [8, 1024, 4096], P('layer'), may hold values from -0.29882812 to 0.29882812
- decoders: bfloat16 [8, 8, 512, 4096], P('layer', None, 'lat'), may hold values from -0.59765625 to 0.59765625
- inputs: bfloat16 [8, 1024, 4096], P('layer'), may hold values from -0.3984375 to 0.3984375
Outputs:
- decoder_grad: bfloat16 [8, 8, 512, 4096], P('layer', None, 'lat')
- code_grad: float32 [8, 512, 1024], P('layer', 'lat')
- encoder_grad: bfloat16 [8, 512, 4096], P('layer', 'lat')
The draws below stay inside these ranges and needn't reach their ends.
All inputs are finite; a program needn't handle non-finite values. No bound on the sum of `relu_mask` on one device may be relied on, other than what follows from the above.
Results may differ from the reference program's by a relative error of at most 0.0049.
Values may be sent and summed in bfloat16 or wider, within the bound.
A program may use at most 128 MiB of HBM per device.

```python
import math
import jax
import jax.numpy as jnp
from jax import lax

D = 4096
LATENTS = 512
TOKENS = 1024
LAYERS = 8


def touch_ends(array, own_key, low, largest):
    shape = array.shape
    spot = [jax.random.randint(jax.random.fold_in(own_key, axis), (), 0, shape[axis]) for axis in range(len(shape))]
    array = array.at[tuple(spot)].set(low)
    longest = shape.index(max(shape))
    spot[longest] = (spot[longest] + 1) % shape[longest]
    return array.at[tuple(spot)].set(largest)


def spiked(result, own_key, source, target, parts, factor):
    owner, partner = [(jnp.arange(result.shape[position]) // (result.shape[position] // parts)).reshape([-1 if axis == position else 1 for axis in range(result.ndim)]) for position in (source, target)]
    chosen = jax.random.permutation(own_key, parts)[partner]
    strong = (owner == chosen) | (owner == (partner + parts // 2) % parts)
    return jnp.where(strong, factor * result, result)


def steps_of(own_key, shape, shards, least, largest):
    factor_of = 1.0
    for dim, parts in shards:
        draws = jax.random.uniform(jax.random.fold_in(jax.random.fold_in(own_key, 6), dim), (parts,), jnp.float32, least / len(shards), largest / len(shards))
        factor_of = factor_of * jnp.repeat(jnp.exp(draws), shape[dim] // parts).reshape((-1,) + (1,) * (len(shape) - 1 - dim))
    return factor_of


def scatter_about(own_key, dims, spread, limit, pieces=(), held_as=jnp.bfloat16):
    level = steps_of(own_key, dims, pieces, -0.22, 0.18) if pieces else 1.0
    result = jax.random.normal(own_key, dims, jnp.float32) * spread * level
    return jnp.minimum(jnp.maximum(result, -limit), limit).astype(held_as)


def gaussian_with(stream_key, shape, deviation, limit, shards, heavy, held_as=jnp.bfloat16):
    entries = deviation * jax.random.normal(stream_key, shape, jnp.float32)
    if shards:
        entries = entries * steps_of(stream_key, shape, shards, -0.22, 0.18)
    return jnp.clip(spiked(entries, jax.random.fold_in(stream_key, 3), *heavy), -limit, limit).astype(held_as)


def setup_inputs(seed: int = 0) -> dict:
    splits = jax.random.split(jax.random.key(seed), 6)
    saved_codes = jnp.clip(jnp.exp(math.log(2.0) - 3.6927934 * jax.random.uniform(splits[0], (LAYERS, LATENTS, TOKENS), jnp.float32) ** steps_of(splits[0], (LAYERS, LATENTS, TOKENS), ((0, 8), (1, 4)), -0.2, 0.2)), 0.049804688, 2.0).astype(jnp.bfloat16)
    relu_mask = touch_ends((jax.random.randint(splits[1], (LAYERS, LATENTS, TOKENS), 0, 2) < 1).astype(jnp.int32), jax.random.fold_in(splits[1], 1), 0, 1)
    errors = scatter_about(splits[2], (LAYERS, TOKENS, D), 0.05, 0.29882812, ((0, 8),))
    decoders = gaussian_with(splits[3], (LAYERS, LAYERS, LATENTS, D), 0.1, 0.59765625, ((0, 8), (2, 4)), (0, 1, 8, 2.0))
    inputs = scatter_about(splits[4], (LAYERS, TOKENS, D), 0.0625, 0.3984375, ((0, 8),))
    return {"saved_codes": saved_codes, "relu_mask": relu_mask, "errors": errors, "decoders": decoders, "inputs": inputs}


def reference(saved_codes, relu_mask, errors, decoders, inputs):
    active = saved_codes * relu_mask.astype(jnp.bfloat16)
    flat_active = active.reshape(LAYERS * LATENTS, TOKENS)
    sources = jnp.arange(LAYERS, dtype=jnp.int32)

    def per_target(running, packed):
        target, target_error, decoder_rows = packed
        allowed = (sources <= target)[:, None, None]
        products = jnp.dot(flat_active, target_error, preferred_element_type=jnp.float32).reshape(LAYERS, LATENTS, D)
        products = jnp.where(allowed, products, 0.0).astype(jnp.bfloat16)
        terms = lax.dot_general(decoder_rows.reshape(LAYERS * LATENTS, D), target_error, (((1,), (1,)), ((), ())), preferred_element_type=jnp.float32).reshape(LAYERS, LATENTS, TOKENS)
        return running + jnp.where(allowed, terms, 0.0), products

    start_sum = jnp.zeros((LAYERS, LATENTS, TOKENS), jnp.float32)
    code_grad, decoder_grad = lax.scan(per_target, start_sum, (sources, errors, decoders))
    pre_grad = (code_grad * relu_mask.astype(jnp.float32)).astype(jnp.bfloat16)
    encoder_grad = jnp.einsum("lfn,lnd->lfd", pre_grad.astype(jnp.float32), inputs.astype(jnp.float32)).astype(jnp.bfloat16)
    return decoder_grad, code_grad, encoder_grad
```

```python
import functools

import jax
import jax.numpy as jnp
from jax import lax
from jax.experimental import pallas as pl
from jax.experimental.pallas import tpu as pltpu
from jax.sharding import PartitionSpec as P

MESH = pl.DeviceIdType.MESH
CHUNKS = 4
DEPTHS = 4
MIB = 1 << 20


def exchange_kernel(
    n, codes_hbm, mask_hbm, errors_hbm, decoders_hbm, gathered, code_grad,
    codes, mask, active, errors, decoders, terms, twin_terms, outgoing, incoming,
    load_sem, decoder_sem, error_sem, own_sem,
    gather_send, gather_recv, relay_send, relay_recv,
    twin_send, twin_recv, term_send, term_recv,
):
    me = lax.axis_index("layer")
    core = lax.rem(me, 2)
    chip = me // 2
    twin = me + 1 - 2 * core
    chips = n // 2
    latents, tokens = active.shape
    width = errors.shape[1]
    token_chunk = tokens // CHUNKS
    depth = width // DEPTHS

    load_codes = pltpu.make_async_copy(codes_hbm, codes, load_sem.at[0])
    load_mask = pltpu.make_async_copy(mask_hbm, mask, load_sem.at[1])

    def load_errors(j):
        rows = pl.ds(pl.multiple_of(j * token_chunk, token_chunk), token_chunk)
        return pltpu.make_async_copy(errors_hbm.at[rows], errors.at[rows], error_sem.at[j])

    def load_decoders(k):
        columns = pl.ds(k * depth, depth)
        return pltpu.make_async_copy(decoders_hbm.at[:, columns], decoders.at[:, columns], decoder_sem.at[k])

    load_codes.start()
    load_mask.start()
    load_errors(0).start()
    for k in range(DEPTHS):
        load_decoders(k).start()
    for j in range(1, CHUNKS):
        load_errors(j).start()

    barrier = pltpu.get_barrier_semaphore()
    pl.semaphore_signal(barrier, inc=1, device_id={"layer": twin}, device_id_type=MESH)
    for other in range(chips):
        @pl.when(other != chip)
        def _():
            pl.semaphore_signal(barrier, inc=1, device_id={"layer": 2 * other + core}, device_id_type=MESH)

    load_codes.wait()
    load_mask.wait()
    active[...] = codes[...] * mask[...].astype(jnp.bfloat16)
    keep = pltpu.make_async_copy(active, gathered.at[me], own_sem)
    keep.start()
    pl.semaphore_wait(barrier, chips)

    def send_active(other):
        return pltpu.make_async_remote_copy(
            src_ref=active, dst_ref=gathered.at[me],
            send_sem=gather_send.at[other], recv_sem=gather_recv.at[chip],
            device_id={"layer": 2 * other + core}, device_id_type=MESH,
        )

    def take_active(source):
        return pltpu.make_async_remote_copy(
            src_ref=active, dst_ref=gathered.at[2 * source + core],
            send_sem=gather_send.at[source], recv_sem=gather_recv.at[source],
            device_id={"layer": 2 * source + core}, device_id_type=MESH,
        )

    def relay(source):
        place = gathered.at[2 * source + core]
        return pltpu.make_async_remote_copy(
            src_ref=place, dst_ref=place,
            send_sem=relay_send.at[source], recv_sem=relay_recv.at[source],
            device_id={"layer": twin}, device_id_type=MESH,
        )

    def take_relay(source):
        place = gathered.at[2 * source + 1 - core]
        return pltpu.make_async_remote_copy(
            src_ref=place, dst_ref=place,
            send_sem=relay_send.at[source], recv_sem=relay_recv.at[source],
            device_id={"layer": twin}, device_id_type=MESH,
        )

    own_to_twin = pltpu.make_async_remote_copy(
        src_ref=active, dst_ref=gathered.at[me],
        send_sem=relay_send.at[chip], recv_sem=relay_recv.at[chip],
        device_id={"layer": twin}, device_id_type=MESH,
    )
    for other in reversed(range(chips)):
        @pl.when(other > chip)
        def _():
            send_active(other).start()

    own_to_twin.start()

    def send_twin(j):
        return pltpu.make_async_remote_copy(
            src_ref=terms.at[j, 1 - core], dst_ref=twin_terms.at[j],
            send_sem=twin_send.at[j], recv_sem=twin_recv.at[j],
            device_id={"layer": twin}, device_id_type=MESH,
        )

    def send_term(j, other):
        return pltpu.make_async_remote_copy(
            src_ref=outgoing.at[j, other], dst_ref=incoming.at[j, chip],
            send_sem=term_send.at[j, other], recv_sem=term_recv.at[j, chip],
            device_id={"layer": 2 * other + core}, device_id_type=MESH,
        )

    def take_term(j, source):
        return pltpu.make_async_remote_copy(
            src_ref=outgoing.at[j, source], dst_ref=incoming.at[j, source],
            send_sem=term_send.at[j, source], recv_sem=term_recv.at[j, source],
            device_id={"layer": 2 * source + core}, device_id_type=MESH,
        )

    def pair_sum(j):
        send_twin(j).wait_recv()
        for other in range(chips):
            @pl.when(other < chip)
            def _():
                total = terms[j, core, other] + twin_terms[j, other]
                outgoing[j, other] = total.astype(jnp.bfloat16)
                send_term(j, other).start()

    @pl.loop(0, CHUNKS)
    def _(j):
        load_errors(j).wait()
        rows = pl.ds(pl.multiple_of(j * token_chunk, token_chunk), token_chunk)
        for k in range(DEPTHS):
            @pl.when(j == 0)
            def _():
                load_decoders(k).wait()
            columns = pl.ds(k * depth, depth)
            product = lax.dot_general(
                decoders[:, columns], errors[rows, columns],
                (((1,), (1,)), ((), ())),
                preferred_element_type=jnp.float32,
            ).reshape(chips, 2, latents, token_chunk)
            for parity in range(2):
                if k == 0:
                    terms[j, parity] = product[:, parity]
                else:
                    terms[j, parity] += product[:, parity]
        send_twin(j).start()

        @pl.when(j >= 1)
        def _():
            pair_sum(j - 1)

        @pl.when(j == CHUNKS - 2)
        def _():
            for source in range(chips):
                @pl.when(source == chip - 1)
                def _():
                    take_active(source).wait_recv()
                    relay(source).start()

    for source in range(chips):
        @pl.when(source < chip - 1)
        def _():
            take_active(source).wait_recv()
            relay(source).start()

    pair_sum(CHUNKS - 1)

    for j in range(CHUNKS):
        columns = pl.ds(j * token_chunk, token_chunk)
        own = terms[j, core, chip]
        code_grad[:, columns] = jnp.where(core == 0, own + twin_terms[j, chip], own)
        for source in range(chips):
            @pl.when(source > chip)
            def _():
                take_term(j, source).wait_recv()
                code_grad[:, columns] += incoming[j, source].astype(jnp.float32)

    keep.wait()
    own_to_twin.wait_send()
    take_relay(chip).wait_recv()
    for other in range(chips):
        @pl.when(other < chip)
        def _():
            relay(other).wait_send()
            take_relay(other).wait_recv()
            for j in range(CHUNKS):
                send_term(j, other).wait_send()

        @pl.when(other > chip)
        def _():
            send_active(other).wait_send()

    for j in range(CHUNKS):
        send_twin(j).wait_send()


def exchange(n, codes, mask, errors, decoders):
    latents, tokens = codes.shape
    width = errors.shape[1]
    chips = n // 2
    token_chunk = tokens // CHUNKS
    any_space = pl.BlockSpec(memory_space=pl.ANY)
    dma = pltpu.SemaphoreType.DMA
    return pl.pallas_call(
        functools.partial(exchange_kernel, n),
        out_shape=(
            jax.ShapeDtypeStruct((n, latents, tokens), jnp.bfloat16),
            jax.ShapeDtypeStruct((latents, tokens), jnp.float32),
        ),
        in_specs=[any_space] * 4,
        out_specs=(any_space, pl.BlockSpec(memory_space=pltpu.VMEM)),
        scratch_shapes=[
            pltpu.VMEM((latents, tokens), jnp.bfloat16),
            pltpu.VMEM((latents, tokens), jnp.int32),
            pltpu.VMEM((latents, tokens), jnp.bfloat16),
            pltpu.VMEM((tokens, width), jnp.bfloat16),
            pltpu.VMEM((n * latents, width), jnp.bfloat16),
            pltpu.VMEM((CHUNKS, 2, chips, latents, token_chunk), jnp.float32),
            pltpu.VMEM((CHUNKS, chips, latents, token_chunk), jnp.float32),
            pltpu.VMEM((CHUNKS, chips, latents, token_chunk), jnp.bfloat16),
            pltpu.VMEM((CHUNKS, chips, latents, token_chunk), jnp.bfloat16),
            dma((2,)), dma((DEPTHS,)), dma((CHUNKS,)), dma,
            dma((chips,)), dma((chips,)), dma((chips,)), dma((chips,)),
            dma((CHUNKS,)), dma((CHUNKS,)), dma((CHUNKS, chips)), dma((CHUNKS, chips)),
        ],
        compiler_params=pltpu.CompilerParams(
            collective_id=0, has_side_effects=True, vmem_limit_bytes=48 * MIB
        ),
        cost_estimate=pl.CostEstimate(
            flops=2 * n * latents * tokens * width,
            bytes_accessed=2 * (n * latents + tokens) * width,
            transcendentals=0,
        ),
        name="exchange",
    )(codes, mask, errors, decoders)


def gradients_kernel(n, gathered, code, mask, errors, inputs, decoder_grad, code_grad, encoder_grad, pre):
    me = lax.axis_index("layer")
    latents = code.shape[0]
    columns = errors.shape[1]
    half = n // 2

    @pl.when(pl.program_id(0) == 0)
    def _():
        code_grad[...] = code[...]
        pre[...] = (code[...] * mask[...].astype(jnp.float32)).astype(jnp.bfloat16)

    def rows(first):
        products = jnp.dot(
            gathered[pl.ds(first * latents, half * latents)], errors[...],
            preferred_element_type=jnp.float32,
        ).reshape(half, latents, columns)
        for s in range(half):
            allowed = first + s <= me
            decoder_grad[first + s] = jnp.where(allowed, products[s], 0.0).astype(jnp.bfloat16)

    rows(0)

    @pl.when(me >= half)
    def _():
        rows(half)

    @pl.when(me < half)
    def _():
        decoder_grad[half:] = jnp.zeros((n - half, latents, columns), jnp.bfloat16)

    encoder_grad[...] = jnp.dot(
        pre[...], inputs[...], preferred_element_type=jnp.float32
    ).astype(jnp.bfloat16)


def gradients(n, gathered, code, mask, errors, inputs):
    latents, tokens = code.shape
    width = errors.shape[1]
    columns = min(512, width)
    whole = lambda *shape: pl.BlockSpec(shape, lambda i: (0,) * len(shape))
    return pl.pallas_call(
        functools.partial(gradients_kernel, n),
        grid=(width // columns,),
        out_shape=(
            jax.ShapeDtypeStruct((n, latents, width), jnp.bfloat16),
            jax.ShapeDtypeStruct((latents, tokens), jnp.float32),
            jax.ShapeDtypeStruct((latents, width), jnp.bfloat16),
        ),
        in_specs=[
            whole(n * latents, tokens),
            whole(latents, tokens),
            whole(latents, tokens),
            pl.BlockSpec((tokens, columns), lambda i: (0, i)),
            pl.BlockSpec((tokens, columns), lambda i: (0, i)),
        ],
        out_specs=(
            pl.BlockSpec((n, latents, columns), lambda i: (0, 0, i)),
            whole(latents, tokens),
            pl.BlockSpec((latents, columns), lambda i: (0, i)),
        ),
        scratch_shapes=[pltpu.VMEM((latents, tokens), jnp.bfloat16)],
        compiler_params=pltpu.CompilerParams(vmem_limit_bytes=40 * MIB),
        cost_estimate=pl.CostEstimate(
            flops=2 * (n + 1) * latents * tokens * width,
            bytes_accessed=2 * (n * latents + 2 * tokens) * width,
            transcendentals=0,
        ),
        name="gradients",
    )(gathered, code, mask, errors, inputs)


def body(saved_codes, relu_mask, errors, decoders, inputs, n):
    latents = saved_codes.shape[1]
    tokens = saved_codes.shape[2]
    width = errors.shape[2]
    gathered, code = exchange(
        n, saved_codes[0], relu_mask[0], errors[0], decoders.reshape(n * latents, width)
    )
    decoder_grad, code_grad, encoder_grad = gradients(
        n, gathered.reshape(n * latents, tokens), code, relu_mask[0], errors[0], inputs[0]
    )
    return decoder_grad[None], code_grad[None], encoder_grad[None]


def solution(mesh):
    return jax.shard_map(
        functools.partial(body, n=mesh.shape["layer"]),
        mesh=mesh,
        in_specs=(
            P("layer", "lat", None),
            P("layer", "lat", None),
            P("layer", None, None),
            P("layer", None, "lat", None),
            P("layer", None, None),
        ),
        out_specs=(P("layer", None, "lat", None), P("layer", "lat", None), P("layer", "lat", None)),
        check_vma=False,
    )
```

```python
import functools

import jax
import jax.numpy as jnp
from jax import lax
from jax.experimental import pallas as pl
from jax.experimental.pallas import tpu as pltpu
from jax.sharding import PartitionSpec as P

MESH = pl.DeviceIdType.MESH
DEPTHS = 4
COLUMNS = 512
MIB = 1 << 20


def exchange_kernel(
    n, codes_hbm, mask_hbm, errors_hbm, decoders_hbm, decoder_grad, code_grad,
    codes, mask, gathered, errors, decoders, terms, twin_terms, outgoing, incoming, stage,
    load_sem, decoder_sem, error_sem, stage_sem,
    gather_send, gather_recv, relay_send, relay_recv,
    twin_send, twin_recv, term_send, term_recv,
):
    me = lax.axis_index("layer")
    core = lax.rem(me, 2)
    chip = me // 2
    twin = me + 1 - 2 * core
    chips = n // 2
    group = chips // 2
    late = chip >= group
    _, latents, tokens = gathered.shape
    width = errors.shape[1]
    half_rows = 2 * group * latents
    half_tokens = tokens // 2
    depth = width // DEPTHS

    load_codes = pltpu.make_async_copy(codes_hbm, codes, load_sem.at[0])
    load_mask = pltpu.make_async_copy(mask_hbm, mask, load_sem.at[1])

    def load_errors(k):
        part = (pl.ds(half_tokens, half_tokens), slice(None))
        if k < DEPTHS:
            part = (pl.ds(0, half_tokens), pl.ds(k * depth, depth))
        return pltpu.make_async_copy(errors_hbm.at[part], errors.at[part], error_sem.at[k])

    def load_decoders(k):
        part = (pl.ds(half_rows, half_rows), slice(None))
        if k < DEPTHS:
            part = (pl.ds(0, half_rows), pl.ds(k * depth, depth))
        return pltpu.make_async_copy(decoders_hbm.at[part], decoders.at[part], decoder_sem.at[k])

    load_codes.start()
    load_mask.start()
    for k in range(DEPTHS):
        load_errors(k).start()
        load_decoders(k).start()
    load_errors(DEPTHS).start()

    @pl.when(late)
    def _():
        load_decoders(DEPTHS).start()

    barrier = pltpu.get_barrier_semaphore()
    pl.semaphore_signal(barrier, inc=1, device_id={"layer": twin}, device_id_type=MESH)
    for other in range(chips):
        @pl.when(other != chip)
        def _():
            pl.semaphore_signal(barrier, inc=1, device_id={"layer": 2 * other + core}, device_id_type=MESH)

    load_codes.wait()
    load_mask.wait()
    gathered[me] = codes[...] * mask[...].astype(jnp.bfloat16)
    pl.semaphore_wait(barrier, chips)

    def send_active(other):
        return pltpu.make_async_remote_copy(
            src_ref=gathered.at[me], dst_ref=gathered.at[me],
            send_sem=gather_send.at[other], recv_sem=gather_recv.at[chip],
            device_id={"layer": 2 * other + core}, device_id_type=MESH,
        )

    def take_active(source):
        place = gathered.at[2 * source + core]
        return pltpu.make_async_remote_copy(
            src_ref=place, dst_ref=place,
            send_sem=gather_send.at[source], recv_sem=gather_recv.at[source],
            device_id={"layer": 2 * source + core}, device_id_type=MESH,
        )

    def relay(source):
        place = gathered.at[2 * source + core]
        return pltpu.make_async_remote_copy(
            src_ref=place, dst_ref=place,
            send_sem=relay_send.at[source], recv_sem=relay_recv.at[source],
            device_id={"layer": twin}, device_id_type=MESH,
        )

    def take_relay(source):
        place = gathered.at[2 * source + 1 - core]
        return pltpu.make_async_remote_copy(
            src_ref=place, dst_ref=place,
            send_sem=relay_send.at[source], recv_sem=relay_recv.at[source],
            device_id={"layer": twin}, device_id_type=MESH,
        )

    for other in reversed(range(chips)):
        @pl.when(other > chip)
        def _():
            send_active(other).start()

    relay(chip).start()

    def send_twin(m):
        return pltpu.make_async_remote_copy(
            src_ref=terms.at[m, 1 - core], dst_ref=twin_terms.at[m],
            send_sem=twin_send.at[m], recv_sem=twin_recv.at[m],
            device_id={"layer": twin}, device_id_type=MESH,
        )

    def send_term(m, place):
        target = (m // 2) * group + place
        return pltpu.make_async_remote_copy(
            src_ref=outgoing.at[m, place], dst_ref=incoming.at[lax.rem(m, 2), chip],
            send_sem=term_send.at[m, place], recv_sem=term_recv.at[lax.rem(m, 2), chip],
            device_id={"layer": 2 * target + core}, device_id_type=MESH,
        )

    def take_term(q, source):
        return pltpu.make_async_remote_copy(
            src_ref=incoming.at[q, source], dst_ref=incoming.at[q, source],
            send_sem=term_send.at[0, 0], recv_sem=term_recv.at[q, source],
            device_id={"layer": 2 * source + core}, device_id_type=MESH,
        )

    def pair_sum(m):
        send_twin(m).wait_recv()
        for place in range(group):
            @pl.when((m // 2) * group + place < chip)
            def _():
                total = terms[m, core, place] + twin_terms[m, place]
                outgoing[m, place] = total.astype(jnp.bfloat16)
                send_term(m, place).start()

    steps = jnp.where(late, 4, 2)

    @pl.loop(0, steps)
    def _(m):
        @pl.when(m == 1)
        def _():
            load_errors(DEPTHS).wait()

        @pl.when(m == 2)
        def _():
            load_decoders(DEPTHS).wait()

        rows = pl.ds(pl.multiple_of((m // 2) * half_rows, half_rows), half_rows)
        part = pl.ds(pl.multiple_of(lax.rem(m, 2) * half_tokens, half_tokens), half_tokens)
        for k in range(DEPTHS):
            @pl.when(m == 0)
            def _():
                load_errors(k).wait()
                load_decoders(k).wait()

            columns = pl.ds(k * depth, depth)
            product = lax.dot_general(
                decoders[rows, columns], errors[part, columns],
                (((1,), (1,)), ((), ())),
                preferred_element_type=jnp.float32,
            ).reshape(group, 2, latents, half_tokens)
            for parity in range(2):
                if k == 0:
                    terms[m, parity] = product[:, parity]
                else:
                    terms[m, parity] += product[:, parity]
        send_twin(m).start()

        @pl.when(m >= 1)
        def _():
            pair_sum(m - 1)

        @pl.when(m == 1)
        def _():
            for source in range(chips):
                @pl.when(source == chip - 1)
                def _():
                    take_active(source).wait_recv()
                    relay(source).start()

    blocks = width // COLUMNS

    def put(first, i, slot):
        columns = pl.ds(pl.multiple_of(i * COLUMNS, COLUMNS), COLUMNS)
        return pltpu.make_async_copy(
            stage.at[slot], decoder_grad.at[pl.ds(first, 2 * group), :, columns], stage_sem.at[slot]
        )

    def decoder_rows(first, late_sum):
        @pl.loop(0, blocks)
        def _(i):
            slot = lax.rem(i, 2)

            @pl.when(i >= 2)
            def _():
                put(first, i - 2, slot).wait()

            columns = pl.ds(pl.multiple_of(i * COLUMNS, COLUMNS), COLUMNS)
            products = jnp.dot(
                gathered[first:first + 2 * group].reshape(half_rows, tokens), errors[:, columns],
                preferred_element_type=jnp.float32,
            ).reshape(2 * group, latents, COLUMNS)
            for s in range(2 * group):
                stage[slot, s] = jnp.where(first + s <= me, products[s], 0.0).astype(jnp.bfloat16)
            put(first, i, slot).start()
            if late_sum:
                @pl.when(i == 0)
                def _():
                    pair_sum(3)

        put(first, blocks - 2, (blocks - 2) % 2).wait()
        put(first, blocks - 1, (blocks - 1) % 2).wait()

    @pl.when(jnp.logical_not(late))
    def _():
        pair_sum(1)
        stage[0] = jnp.zeros(stage.shape[1:], stage.dtype)
        for i in range(blocks):
            put(2 * group, i, 0).start()

    for source in range(chips):
        @pl.when(source < chip - 1)
        def _():
            take_active(source).wait_recv()
            relay(source).start()

    take_relay(chip).wait_recv()

    @pl.when(late)
    def _():
        for source in range(group, chips):
            @pl.when(source < chip)
            def _():
                take_relay(source).wait_recv()
        decoder_rows(2 * group, True)

    @pl.when(jnp.logical_not(late))
    def _():
        for i in range(blocks):
            put(2 * group, i, 0).wait()

    for source in range(group):
        @pl.when(source < chip)
        def _():
            take_relay(source).wait_recv()
    decoder_rows(0, False)

    half = chip // group
    place = lax.rem(chip, group)
    for q in range(2):
        columns = pl.ds(q * half_tokens, half_tokens)
        own = terms[2 * half + q, core, place]
        code_grad[:, columns] = jnp.where(core == 0, own + twin_terms[2 * half + q, place], own)
        for source in range(chips):
            @pl.when(source > chip)
            def _():
                take_term(q, source).wait_recv()
                code_grad[:, columns] += incoming[q, source].astype(jnp.float32)

    relay(chip).wait_send()
    for other in range(chips):
        @pl.when(other < chip)
        def _():
            relay(other).wait_send()
            for q in range(2):
                send_term(2 * (other // group) + q, other % group).wait_send()

        @pl.when(other > chip)
        def _():
            send_active(other).wait_send()

    for m in range(2):
        send_twin(m).wait_send()

    @pl.when(late)
    def _():
        for m in range(2, 4):
            send_twin(m).wait_send()


def exchange(n, codes, mask, errors, decoders):
    latents, tokens = codes.shape
    width = errors.shape[1]
    chips = n // 2
    group = chips // 2
    half_tokens = tokens // 2
    any_space = pl.BlockSpec(memory_space=pl.ANY)
    dma = pltpu.SemaphoreType.DMA
    return pl.pallas_call(
        functools.partial(exchange_kernel, n),
        out_shape=(
            jax.ShapeDtypeStruct((n, latents, width), jnp.bfloat16),
            jax.ShapeDtypeStruct((latents, tokens), jnp.float32),
        ),
        in_specs=[any_space] * 4,
        out_specs=(any_space, pl.BlockSpec(memory_space=pltpu.VMEM)),
        scratch_shapes=[
            pltpu.VMEM((latents, tokens), jnp.bfloat16),
            pltpu.VMEM((latents, tokens), jnp.int32),
            pltpu.VMEM((n, latents, tokens), jnp.bfloat16),
            pltpu.VMEM((tokens, width), jnp.bfloat16),
            pltpu.VMEM((n * latents, width), jnp.bfloat16),
            pltpu.VMEM((4, 2, group, latents, half_tokens), jnp.float32),
            pltpu.VMEM((4, group, latents, half_tokens), jnp.float32),
            pltpu.VMEM((4, group, latents, half_tokens), jnp.bfloat16),
            pltpu.VMEM((2, chips, latents, half_tokens), jnp.bfloat16),
            pltpu.VMEM((2, 2 * group, latents, COLUMNS), jnp.bfloat16),
            dma((2,)), dma((DEPTHS + 1,)), dma((DEPTHS + 1,)), dma((2,)),
            dma((chips,)), dma((chips,)), dma((chips,)), dma((chips,)),
            dma((4,)), dma((4,)), dma((4, group)), dma((2, chips)),
        ],
        compiler_params=pltpu.CompilerParams(
            collective_id=0, has_side_effects=True, vmem_limit_bytes=38 * MIB
        ),
        cost_estimate=pl.CostEstimate(
            flops=4 * n * latents * tokens * width,
            bytes_accessed=2 * (2 * n * latents + tokens) * width,
            transcendentals=0,
        ),
        name="exchange",
    )(codes, mask, errors, decoders)


def encoder_kernel(held, code, mask, inputs, decoder_grad, code_grad, encoder_grad, pre, pass_sem):
    def hand_on(s):
        return pltpu.make_async_copy(held.at[s], decoder_grad.at[s], pass_sem.at[s])

    @pl.when(pl.program_id(0) == 0)
    def _():
        for s in range(held.shape[0]):
            hand_on(s).start()
        code_grad[...] = code[...]
        pre[...] = (code[...] * mask[...].astype(jnp.float32)).astype(jnp.bfloat16)

    encoder_grad[...] = jnp.dot(
        pre[...], inputs[...], preferred_element_type=jnp.float32
    ).astype(jnp.bfloat16)

    @pl.when(pl.program_id(0) == pl.num_programs(0) - 1)
    def _():
        for s in range(held.shape[0]):
            hand_on(s).wait()


def encoder(held, code, mask, inputs):
    latents, tokens = code.shape
    n, _, width = held.shape
    whole = lambda *shape: pl.BlockSpec(shape, lambda i: (0,) * len(shape))
    any_space = pl.BlockSpec(memory_space=pl.ANY)
    return pl.pallas_call(
        encoder_kernel,
        grid=(width // COLUMNS,),
        out_shape=(
            jax.ShapeDtypeStruct(held.shape, jnp.bfloat16),
            jax.ShapeDtypeStruct((latents, tokens), jnp.float32),
            jax.ShapeDtypeStruct((latents, width), jnp.bfloat16),
        ),
        in_specs=[
            any_space,
            whole(latents, tokens),
            whole(latents, tokens),
            pl.BlockSpec((tokens, COLUMNS), lambda i: (0, i)),
        ],
        out_specs=(
            any_space,
            whole(latents, tokens),
            pl.BlockSpec((latents, COLUMNS), lambda i: (0, i)),
        ),
        scratch_shapes=[
            pltpu.VMEM((latents, tokens), jnp.bfloat16),
            pltpu.SemaphoreType.DMA((n,)),
        ],
        compiler_params=pltpu.CompilerParams(vmem_limit_bytes=20 * MIB),
        cost_estimate=pl.CostEstimate(
            flops=2 * latents * tokens * width,
            bytes_accessed=2 * (2 * n * latents + tokens) * width,
            transcendentals=0,
        ),
        name="encoder",
    )(held, code, mask, inputs)


def body(saved_codes, relu_mask, errors, decoders, inputs, n):
    latents = saved_codes.shape[1]
    width = errors.shape[2]
    held, code = exchange(
        n, saved_codes[0], relu_mask[0], errors[0], decoders.reshape(n * latents, width)
    )
    decoder_grad, code_grad, encoder_grad = encoder(held, code, relu_mask[0], inputs[0])
    return decoder_grad[None], code_grad[None], encoder_grad[None]


def solution(mesh):
    return jax.shard_map(
        functools.partial(body, n=mesh.shape["layer"]),
        mesh=mesh,
        in_specs=(
            P("layer", "lat", None),
            P("layer", "lat", None),
            P("layer", None, None),
            P("layer", None, "lat", None),
            P("layer", None, None),
        ),
        out_specs=(P("layer", None, "lat", None), P("layer", "lat", None), P("layer", "lat", None)),
        check_vma=False,
    )
```

```python
import functools

import jax
import jax.numpy as jnp
from jax import lax
from jax.experimental import pallas as pl
from jax.experimental.pallas import tpu as pltpu
from jax.sharding import PartitionSpec as P

MESH = pl.DeviceIdType.MESH
DEPTHS = 4
COLUMNS = 512
MIB = 1 << 20


def exchange_kernel(
    n, codes_hbm, mask_hbm, errors_hbm, decoders_hbm, inputs_hbm, decoder_grad, code_grad, encoder_grad,
    codes, mask, gathered, errors, slab, terms, twin_terms, outgoing, incoming, stage, pre,
    load_sem, decoder_sem, error_sem, stage_sem,
    gather_send, gather_recv, relay_send, relay_recv,
    twin_send, twin_recv, term_send, term_recv,
):
    me = lax.axis_index("layer")
    core = lax.rem(me, 2)
    chip = me // 2
    twin = me + 1 - 2 * core
    chips = n // 2
    group = chips // 2
    late = chip >= group
    _, latents, tokens = gathered.shape
    width = errors.shape[1]
    decoders = slab.at[pl.ds(0, n * latents)]
    inputs = slab.at[pl.ds(0, tokens)]
    half_rows = 2 * group * latents
    half_tokens = tokens // 2
    depth = width // DEPTHS

    load_codes = pltpu.make_async_copy(codes_hbm, codes, load_sem.at[0])
    load_mask = pltpu.make_async_copy(mask_hbm, mask, load_sem.at[1])
    load_inputs = pltpu.make_async_copy(inputs_hbm, inputs, load_sem.at[2])

    def load_errors(k):
        part = (pl.ds(half_tokens, half_tokens), slice(None))
        if k < DEPTHS:
            part = (pl.ds(0, half_tokens), pl.ds(k * depth, depth))
        return pltpu.make_async_copy(errors_hbm.at[part], errors.at[part], error_sem.at[k])

    def load_decoders(k):
        part = (pl.ds(half_rows, half_rows), slice(None))
        if k < DEPTHS:
            part = (pl.ds(0, half_rows), pl.ds(k * depth, depth))
        return pltpu.make_async_copy(decoders_hbm.at[part], decoders.at[part], decoder_sem.at[k])

    load_codes.start()
    load_mask.start()
    for k in range(DEPTHS):
        load_errors(k).start()
        load_decoders(k).start()
    load_errors(DEPTHS).start()

    @pl.when(late)
    def _():
        load_decoders(DEPTHS).start()

    barrier = pltpu.get_barrier_semaphore()
    pl.semaphore_signal(barrier, inc=1, device_id={"layer": twin}, device_id_type=MESH)
    for other in range(chips):
        @pl.when(other != chip)
        def _():
            pl.semaphore_signal(barrier, inc=1, device_id={"layer": 2 * other + core}, device_id_type=MESH)

    load_codes.wait()
    load_mask.wait()
    gathered[me] = codes[...] * mask[...].astype(jnp.bfloat16)
    pl.semaphore_wait(barrier, chips)

    def send_active(other):
        return pltpu.make_async_remote_copy(
            src_ref=gathered.at[me], dst_ref=gathered.at[me],
            send_sem=gather_send.at[other], recv_sem=gather_recv.at[chip],
            device_id={"layer": 2 * other + core}, device_id_type=MESH,
        )

    def take_active(source):
        place = gathered.at[2 * source + core]
        return pltpu.make_async_remote_copy(
            src_ref=place, dst_ref=place,
            send_sem=gather_send.at[source], recv_sem=gather_recv.at[source],
            device_id={"layer": 2 * source + core}, device_id_type=MESH,
        )

    def relay(source):
        place = gathered.at[2 * source + core]
        return pltpu.make_async_remote_copy(
            src_ref=place, dst_ref=place,
            send_sem=relay_send.at[source], recv_sem=relay_recv.at[source],
            device_id={"layer": twin}, device_id_type=MESH,
        )

    def take_relay(source):
        place = gathered.at[2 * source + 1 - core]
        return pltpu.make_async_remote_copy(
            src_ref=place, dst_ref=place,
            send_sem=relay_send.at[source], recv_sem=relay_recv.at[source],
            device_id={"layer": twin}, device_id_type=MESH,
        )

    for other in reversed(range(chips)):
        @pl.when(other > chip)
        def _():
            send_active(other).start()

    relay(chip).start()

    def send_twin(m):
        return pltpu.make_async_remote_copy(
            src_ref=terms.at[m, 1 - core], dst_ref=twin_terms.at[m],
            send_sem=twin_send.at[m], recv_sem=twin_recv.at[m],
            device_id={"layer": twin}, device_id_type=MESH,
        )

    def send_term(m, place):
        target = (m // 2) * group + place
        return pltpu.make_async_remote_copy(
            src_ref=outgoing.at[m, place], dst_ref=incoming.at[lax.rem(m, 2), chip],
            send_sem=term_send.at[m, place], recv_sem=term_recv.at[lax.rem(m, 2), chip],
            device_id={"layer": 2 * target + core}, device_id_type=MESH,
        )

    def take_term(q, source):
        return pltpu.make_async_remote_copy(
            src_ref=incoming.at[q, source], dst_ref=incoming.at[q, source],
            send_sem=term_send.at[0, 0], recv_sem=term_recv.at[q, source],
            device_id={"layer": 2 * source + core}, device_id_type=MESH,
        )

    def pair_sum(m):
        send_twin(m).wait_recv()
        for place in range(group):
            @pl.when((m // 2) * group + place < chip)
            def _():
                total = terms[m, core, place] + twin_terms[m, place]
                outgoing[m, place] = total.astype(jnp.bfloat16)
                send_term(m, place).start()

    steps = jnp.where(late, 4, 2)

    @pl.loop(0, steps)
    def _(m):
        @pl.when(m == 1)
        def _():
            load_errors(DEPTHS).wait()

        @pl.when(m == 2)
        def _():
            load_decoders(DEPTHS).wait()

        rows = pl.ds(pl.multiple_of((m // 2) * half_rows, half_rows), half_rows)
        part = pl.ds(pl.multiple_of(lax.rem(m, 2) * half_tokens, half_tokens), half_tokens)
        for k in range(DEPTHS):
            @pl.when(m == 0)
            def _():
                load_errors(k).wait()
                load_decoders(k).wait()

            columns = pl.ds(k * depth, depth)
            product = lax.dot_general(
                decoders[rows, columns], errors[part, columns],
                (((1,), (1,)), ((), ())),
                preferred_element_type=jnp.float32,
            ).reshape(group, 2, latents, half_tokens)
            for parity in range(2):
                if k == 0:
                    terms[m, parity] = product[:, parity]
                else:
                    terms[m, parity] += product[:, parity]
        send_twin(m).start()

        @pl.when(m >= 1)
        def _():
            pair_sum(m - 1)

        @pl.when(m == 1)
        def _():
            for source in range(chips):
                @pl.when(source == chip - 1)
                def _():
                    take_active(source).wait_recv()
                    relay(source).start()

    load_inputs.start()

    blocks = width // COLUMNS

    def put(first, i, slot):
        columns = pl.ds(pl.multiple_of(i * COLUMNS, COLUMNS), COLUMNS)
        return pltpu.make_async_copy(
            stage.at[slot], decoder_grad.at[pl.ds(first, 2 * group), :, columns], stage_sem.at[slot]
        )

    def relay_far():
        for source in range(group):
            @pl.when(source < chip - 1)
            def _():
                take_active(source).wait_recv()
                relay(source).start()

    def decoder_rows(first, near):
        @pl.loop(0, blocks)
        def _(i):
            slot = lax.rem(i, 2)

            @pl.when(i >= 2)
            def _():
                put(first, i - 2, slot).wait()

            columns = pl.ds(pl.multiple_of(i * COLUMNS, COLUMNS), COLUMNS)
            products = jnp.dot(
                gathered[first:first + 2 * group].reshape(half_rows, tokens), errors[:, columns],
                preferred_element_type=jnp.float32,
            ).reshape(2 * group, latents, COLUMNS)
            for s in range(2 * group):
                stage[slot, s] = jnp.where(first + s <= me, products[s], 0.0).astype(jnp.bfloat16)
            put(first, i, slot).start()
            if near:
                @pl.when(i == 0)
                def _():
                    pair_sum(3)

                @pl.when(i == blocks - 3)
                def _():
                    relay_far()

        put(first, blocks - 2, (blocks - 2) % 2).wait()
        put(first, blocks - 1, (blocks - 1) % 2).wait()

    @pl.when(jnp.logical_not(late))
    def _():
        pair_sum(1)
        stage[0] = jnp.zeros(stage.shape[1:], stage.dtype)
        for i in range(blocks):
            put(2 * group, i, 0).start()

    take_relay(chip).wait_recv()

    @pl.when(late)
    def _():
        for source in range(group, chips):
            @pl.when(source < chip - 1)
            def _():
                take_active(source).wait_recv()
                relay(source).start()

        for source in range(group, chips):
            @pl.when(source < chip)
            def _():
                take_relay(source).wait_recv()
        decoder_rows(2 * group, True)

    @pl.when(jnp.logical_not(late))
    def _():
        relay_far()
        for i in range(blocks):
            put(2 * group, i, 0).wait()

    for source in range(group):
        @pl.when(source < chip)
        def _():
            take_relay(source).wait_recv()
    decoder_rows(0, False)

    half = chip // group
    place = lax.rem(chip, group)
    for q in range(2):
        columns = pl.ds(q * half_tokens, half_tokens)
        own = terms[2 * half + q, core, place]
        code_grad[:, columns] = jnp.where(core == 0, own + twin_terms[2 * half + q, place], own)
        for source in range(chips):
            @pl.when(source > chip)
            def _():
                take_term(q, source).wait_recv()
                code_grad[:, columns] += incoming[q, source].astype(jnp.float32)

    pre[...] = (code_grad[...] * mask[...].astype(jnp.float32)).astype(jnp.bfloat16)
    load_inputs.wait()

    @pl.loop(0, blocks)
    def _(i):
        columns = pl.ds(pl.multiple_of(i * COLUMNS, COLUMNS), COLUMNS)
        encoder_grad[:, columns] = jnp.dot(
            pre[...], inputs[:, columns], preferred_element_type=jnp.float32
        ).astype(jnp.bfloat16)

    relay(chip).wait_send()
    for other in range(chips):
        @pl.when(other < chip)
        def _():
            relay(other).wait_send()
            for q in range(2):
                send_term(2 * (other // group) + q, other % group).wait_send()

        @pl.when(other > chip)
        def _():
            send_active(other).wait_send()

    for m in range(2):
        send_twin(m).wait_send()

    @pl.when(late)
    def _():
        for m in range(2, 4):
            send_twin(m).wait_send()


def exchange(n, codes, mask, errors, decoders, inputs):
    latents, tokens = codes.shape
    width = errors.shape[1]
    chips = n // 2
    group = chips // 2
    half_tokens = tokens // 2
    any_space = pl.BlockSpec(memory_space=pl.ANY)
    dma = pltpu.SemaphoreType.DMA
    return pl.pallas_call(
        functools.partial(exchange_kernel, n),
        out_shape=(
            jax.ShapeDtypeStruct((n, latents, width), jnp.bfloat16),
            jax.ShapeDtypeStruct((latents, tokens), jnp.float32),
            jax.ShapeDtypeStruct((latents, width), jnp.bfloat16),
        ),
        in_specs=[any_space] * 5,
        out_specs=(any_space,) + (pl.BlockSpec(memory_space=pltpu.VMEM),) * 2,
        scratch_shapes=[
            pltpu.VMEM((latents, tokens), jnp.bfloat16),
            pltpu.VMEM((latents, tokens), jnp.int32),
            pltpu.VMEM((n, latents, tokens), jnp.bfloat16),
            pltpu.VMEM((tokens, width), jnp.bfloat16),
            pltpu.VMEM((max(n * latents, tokens), width), jnp.bfloat16),
            pltpu.VMEM((4, 2, group, latents, half_tokens), jnp.float32),
            pltpu.VMEM((4, group, latents, half_tokens), jnp.float32),
            pltpu.VMEM((4, group, latents, half_tokens), jnp.bfloat16),
            pltpu.VMEM((2, chips, latents, half_tokens), jnp.bfloat16),
            pltpu.VMEM((2, 2 * group, latents, COLUMNS), jnp.bfloat16),
            pltpu.VMEM((latents, tokens), jnp.bfloat16),
            dma((3,)), dma((DEPTHS + 1,)), dma((DEPTHS + 1,)), dma((2,)),
            dma((chips,)), dma((chips,)), dma((chips,)), dma((chips,)),
            dma((4,)), dma((4,)), dma((4, group)), dma((2, chips)),
        ],
        compiler_params=pltpu.CompilerParams(
            collective_id=0, has_side_effects=True, vmem_limit_bytes=40 * MIB
        ),
        cost_estimate=pl.CostEstimate(
            flops=(4 * n + 2) * latents * tokens * width,
            bytes_accessed=2 * (2 * n * latents + tokens) * width,
            transcendentals=0,
        ),
        name="exchange",
    )(codes, mask, errors, decoders, inputs)


def hand_on_kernel(*refs):
    count = (len(refs) - 1) // 2
    sems = refs[-1]
    copies = [pltpu.make_async_copy(refs[i], refs[count + i], sems.at[i]) for i in range(count)]
    for copy in copies:
        copy.start()
    for copy in copies:
        copy.wait()


def hand_on(*arrays):
    any_space = pl.BlockSpec(memory_space=pl.ANY)
    return pl.pallas_call(
        hand_on_kernel,
        out_shape=tuple(jax.ShapeDtypeStruct(a.shape, a.dtype) for a in arrays),
        in_specs=[any_space] * len(arrays),
        out_specs=(any_space,) * len(arrays),
        scratch_shapes=[pltpu.SemaphoreType.DMA((len(arrays),))],
        compiler_params=pltpu.CompilerParams(vmem_limit_bytes=MIB),
        name="hand_on",
    )(*arrays)


def body(saved_codes, relu_mask, errors, decoders, inputs, n):
    latents = saved_codes.shape[1]
    width = errors.shape[2]
    held = exchange(
        n, saved_codes[0], relu_mask[0], errors[0], decoders.reshape(n * latents, width), inputs[0]
    )
    return tuple(result[None] for result in hand_on(*held))


def solution(mesh):
    return jax.shard_map(
        functools.partial(body, n=mesh.shape["layer"]),
        mesh=mesh,
        in_specs=(
            P("layer", "lat", None),
            P("layer", "lat", None),
            P("layer", None, None),
            P("layer", None, "lat", None),
            P("layer", None, None),
        ),
        out_specs=(P("layer", None, "lat", None), P("layer", "lat", None), P("layer", "lat", None)),
        check_vma=False,
    )
```

```python
import functools

import jax
import jax.numpy as jnp
from jax import lax
from jax.experimental import pallas as pl
from jax.experimental.pallas import tpu as pltpu
from jax.sharding import PartitionSpec as P

MESH = pl.DeviceIdType.MESH
DEPTHS = 2
COLUMNS = 512
MIB = 1 << 20


def exchange_kernel(
    n, codes_hbm, mask_hbm, errors_hbm, decoders_hbm, inputs_hbm, decoder_grad, code_grad, encoder_grad,
    codes, mask, gathered, errors, slab, terms, twin_terms, outgoing, incoming, stage, pre,
    load_sem, decoder_sem, error_sem, stage_sem,
    gather_send, gather_recv, relay_send, relay_recv,
    twin_send, twin_recv, term_send, term_recv,
):
    me = lax.axis_index("layer")
    core = lax.rem(me, 2)
    chip = me // 2
    twin = me + 1 - 2 * core
    chips = n // 2
    group = chips // 2
    late = chip >= group
    _, latents, tokens = gathered.shape
    width = errors.shape[1]
    decoders = slab.at[pl.ds(0, n * latents)]
    inputs = slab.at[pl.ds(0, tokens)]
    half_rows = 2 * group * latents
    half_tokens = tokens // 2
    depth = width // DEPTHS

    load_codes = pltpu.make_async_copy(codes_hbm, codes, load_sem.at[0])
    load_mask = pltpu.make_async_copy(mask_hbm, mask, load_sem.at[1])
    load_inputs = pltpu.make_async_copy(inputs_hbm, inputs, load_sem.at[2])

    def load_errors(k):
        part = (pl.ds(half_tokens, half_tokens), slice(None))
        if k < DEPTHS:
            part = (pl.ds(0, half_tokens), pl.ds(k * depth, depth))
        return pltpu.make_async_copy(errors_hbm.at[part], errors.at[part], error_sem.at[k])

    def load_decoders(k):
        part = (slice(None), pl.ds(k * depth, depth))
        return pltpu.make_async_copy(decoders_hbm.at[part], decoders.at[part], decoder_sem.at[k])

    load_codes.start()
    load_mask.start()
    for k in range(DEPTHS):
        load_errors(k).start()
        load_decoders(k).start()
    load_errors(DEPTHS).start()
    barrier = pltpu.get_barrier_semaphore()
    pl.semaphore_signal(barrier, inc=1, device_id={"layer": twin}, device_id_type=MESH)
    for other in range(chips):
        @pl.when(other != chip)
        def _():
            pl.semaphore_signal(barrier, inc=1, device_id={"layer": 2 * other + core}, device_id_type=MESH)

    load_codes.wait()
    load_mask.wait()
    gathered[me] = codes[...] * mask[...].astype(jnp.bfloat16)
    pl.semaphore_wait(barrier, chips)

    def send_active(other):
        return pltpu.make_async_remote_copy(
            src_ref=gathered.at[me], dst_ref=gathered.at[me],
            send_sem=gather_send.at[other], recv_sem=gather_recv.at[chip],
            device_id={"layer": 2 * other + core}, device_id_type=MESH,
        )

    def take_active(source):
        place = gathered.at[2 * source + core]
        return pltpu.make_async_remote_copy(
            src_ref=place, dst_ref=place,
            send_sem=gather_send.at[source], recv_sem=gather_recv.at[source],
            device_id={"layer": 2 * source + core}, device_id_type=MESH,
        )

    def relay(source):
        place = gathered.at[2 * source + core]
        return pltpu.make_async_remote_copy(
            src_ref=place, dst_ref=place,
            send_sem=relay_send.at[source], recv_sem=relay_recv.at[source],
            device_id={"layer": twin}, device_id_type=MESH,
        )

    def take_relay(source):
        place = gathered.at[2 * source + 1 - core]
        return pltpu.make_async_remote_copy(
            src_ref=place, dst_ref=place,
            send_sem=relay_send.at[source], recv_sem=relay_recv.at[source],
            device_id={"layer": twin}, device_id_type=MESH,
        )

    for other in reversed(range(chips)):
        @pl.when(other > chip)
        def _():
            send_active(other).start()

    relay(chip).start()

    def send_twin(m):
        return pltpu.make_async_remote_copy(
            src_ref=terms.at[m, 1 - core], dst_ref=twin_terms.at[m],
            send_sem=twin_send.at[m], recv_sem=twin_recv.at[m],
            device_id={"layer": twin}, device_id_type=MESH,
        )

    def send_term(m, place):
        target = (m // 2) * group + place
        return pltpu.make_async_remote_copy(
            src_ref=outgoing.at[m, place], dst_ref=incoming.at[lax.rem(m, 2), chip],
            send_sem=term_send.at[m, place], recv_sem=term_recv.at[lax.rem(m, 2), chip],
            device_id={"layer": 2 * target + core}, device_id_type=MESH,
        )

    def take_term(q, source):
        return pltpu.make_async_remote_copy(
            src_ref=incoming.at[q, source], dst_ref=incoming.at[q, source],
            send_sem=term_send.at[0, 0], recv_sem=term_recv.at[q, source],
            device_id={"layer": 2 * source + core}, device_id_type=MESH,
        )

    def pair_sum(m):
        send_twin(m).wait_recv()
        for place in range(group):
            @pl.when((m // 2) * group + place < chip)
            def _():
                total = terms[m, core, place] + twin_terms[m, place]
                outgoing[m, place] = total.astype(jnp.bfloat16)
                send_term(m, place).start()

    def products(part, columns):
        return lax.dot_general(
            decoders[:, columns], errors[part, columns],
            (((1,), (1,)), ((), ())),
            preferred_element_type=jnp.float32,
        ).reshape(2, group, 2, latents, half_tokens)

    for q in range(2):
        part = pl.ds(q * half_tokens, half_tokens)
        if q == 0:
            for k in range(DEPTHS):
                load_errors(k).wait()
                load_decoders(k).wait()
                product = products(part, pl.ds(k * depth, depth))
                for half in range(2):
                    for parity in range(2):
                        if k == 0:
                            terms[2 * half, parity] = product[half, :, parity]
                        else:
                            terms[2 * half, parity] += product[half, :, parity]
        else:
            load_errors(DEPTHS).wait()
            product = products(part, slice(None))
            for half in range(2):
                for parity in range(2):
                    terms[2 * half + 1, parity] = product[half, :, parity]
        send_twin(q).start()

        @pl.when(late)
        def _():
            send_twin(2 + q).start()

    pair_sum(0)

    @pl.when(late)
    def _():
        pair_sum(2)

    for source in range(chips):
        @pl.when(source == chip - 1)
        def _():
            take_active(source).wait_recv()
            relay(source).start()

    load_inputs.start()

    blocks = width // COLUMNS

    def put(first, i, slot):
        columns = pl.ds(pl.multiple_of(i * COLUMNS, COLUMNS), COLUMNS)
        return pltpu.make_async_copy(
            stage.at[slot], decoder_grad.at[pl.ds(first, 2 * group), :, columns], stage_sem.at[slot]
        )

    def relay_far():
        for source in range(group):
            @pl.when(source < chip - 1)
            def _():
                take_active(source).wait_recv()
                relay(source).start()

    def decoder_rows(first, near):
        @pl.loop(0, blocks)
        def _(i):
            slot = lax.rem(i, 2)

            @pl.when(i >= 2)
            def _():
                put(first, i - 2, slot).wait()

            columns = pl.ds(pl.multiple_of(i * COLUMNS, COLUMNS), COLUMNS)
            products = jnp.dot(
                gathered[first:first + 2 * group].reshape(half_rows, tokens), errors[:, columns],
                preferred_element_type=jnp.float32,
            ).reshape(2 * group, latents, COLUMNS)
            for s in range(2 * group):
                stage[slot, s] = jnp.where(first + s <= me, products[s], 0.0).astype(jnp.bfloat16)
            put(first, i, slot).start()
            if near:
                @pl.when(i == 0)
                def _():
                    pair_sum(1)
                    pair_sum(3)

                @pl.when(i == blocks - 3)
                def _():
                    relay_far()

        put(first, blocks - 2, (blocks - 2) % 2).wait()
        put(first, blocks - 1, (blocks - 1) % 2).wait()

    @pl.when(jnp.logical_not(late))
    def _():
        pair_sum(1)
        stage[0] = jnp.zeros(stage.shape[1:], stage.dtype)
        for i in range(blocks):
            put(2 * group, i, 0).start()

    take_relay(chip).wait_recv()

    @pl.when(late)
    def _():
        for source in range(group, chips):
            @pl.when(source < chip - 1)
            def _():
                take_active(source).wait_recv()
                relay(source).start()

        for source in range(group, chips):
            @pl.when(source < chip)
            def _():
                take_relay(source).wait_recv()
        decoder_rows(2 * group, True)

    @pl.when(jnp.logical_not(late))
    def _():
        relay_far()
        for i in range(blocks):
            put(2 * group, i, 0).wait()

    for source in range(group):
        @pl.when(source < chip)
        def _():
            take_relay(source).wait_recv()
    decoder_rows(0, False)

    half = chip // group
    place = lax.rem(chip, group)
    for q in range(2):
        columns = pl.ds(q * half_tokens, half_tokens)
        own = terms[2 * half + q, core, place]
        code_grad[:, columns] = jnp.where(core == 0, own + twin_terms[2 * half + q, place], own)
        for source in range(chips):
            @pl.when(source > chip)
            def _():
                take_term(q, source).wait_recv()
                code_grad[:, columns] += incoming[q, source].astype(jnp.float32)

    pre[...] = (code_grad[...] * mask[...].astype(jnp.float32)).astype(jnp.bfloat16)
    load_inputs.wait()

    @pl.loop(0, blocks)
    def _(i):
        columns = pl.ds(pl.multiple_of(i * COLUMNS, COLUMNS), COLUMNS)
        encoder_grad[:, columns] = jnp.dot(
            pre[...], inputs[:, columns], preferred_element_type=jnp.float32
        ).astype(jnp.bfloat16)

    relay(chip).wait_send()
    for other in range(chips):
        @pl.when(other < chip)
        def _():
            relay(other).wait_send()
            for q in range(2):
                send_term(2 * (other // group) + q, other % group).wait_send()

        @pl.when(other > chip)
        def _():
            send_active(other).wait_send()

    for m in range(2):
        send_twin(m).wait_send()

    @pl.when(late)
    def _():
        for m in range(2, 4):
            send_twin(m).wait_send()


def exchange(n, codes, mask, errors, decoders, inputs):
    latents, tokens = codes.shape
    width = errors.shape[1]
    chips = n // 2
    group = chips // 2
    half_tokens = tokens // 2
    any_space = pl.BlockSpec(memory_space=pl.ANY)
    dma = pltpu.SemaphoreType.DMA
    return pl.pallas_call(
        functools.partial(exchange_kernel, n),
        out_shape=(
            jax.ShapeDtypeStruct((n, latents, width), jnp.bfloat16),
            jax.ShapeDtypeStruct((latents, tokens), jnp.float32),
            jax.ShapeDtypeStruct((latents, width), jnp.bfloat16),
        ),
        in_specs=[any_space] * 5,
        out_specs=(any_space,) + (pl.BlockSpec(memory_space=pltpu.VMEM),) * 2,
        scratch_shapes=[
            pltpu.VMEM((latents, tokens), jnp.bfloat16),
            pltpu.VMEM((latents, tokens), jnp.int32),
            pltpu.VMEM((n, latents, tokens), jnp.bfloat16),
            pltpu.VMEM((tokens, width), jnp.bfloat16),
            pltpu.VMEM((max(n * latents, tokens), width), jnp.bfloat16),
            pltpu.VMEM((4, 2, group, latents, half_tokens), jnp.float32),
            pltpu.VMEM((4, group, latents, half_tokens), jnp.float32),
            pltpu.VMEM((4, group, latents, half_tokens), jnp.bfloat16),
            pltpu.VMEM((2, chips, latents, half_tokens), jnp.bfloat16),
            pltpu.VMEM((2, 2 * group, latents, COLUMNS), jnp.bfloat16),
            pltpu.VMEM((latents, tokens), jnp.bfloat16),
            dma((3,)), dma((DEPTHS,)), dma((DEPTHS + 1,)), dma((2,)),
            dma((chips,)), dma((chips,)), dma((chips,)), dma((chips,)),
            dma((4,)), dma((4,)), dma((4, group)), dma((2, chips)),
        ],
        compiler_params=pltpu.CompilerParams(
            collective_id=0, has_side_effects=True, vmem_limit_bytes=40 * MIB
        ),
        cost_estimate=pl.CostEstimate(
            flops=(4 * n + 2) * latents * tokens * width,
            bytes_accessed=2 * (2 * n * latents + tokens) * width,
            transcendentals=0,
        ),
        name="exchange",
    )(codes, mask, errors, decoders, inputs)


def hand_on_kernel(*refs):
    count = (len(refs) - 1) // 2
    sems = refs[-1]
    pieces = []
    for source, target in zip(refs[:count], refs[count:-1]):
        if len(source.shape) == 3:
            pieces += [(source.at[i], target.at[i]) for i in range(source.shape[0])]
        else:
            pieces.append((source, target))
    copies = [pltpu.make_async_copy(*piece, sems.at[i]) for i, piece in enumerate(pieces)]
    for copy in copies:
        copy.start()
    for copy in copies:
        copy.wait()


def hand_on(*arrays):
    any_space = pl.BlockSpec(memory_space=pl.ANY)
    return pl.pallas_call(
        hand_on_kernel,
        out_shape=tuple(jax.ShapeDtypeStruct(a.shape, a.dtype) for a in arrays),
        in_specs=[any_space] * len(arrays),
        out_specs=(any_space,) * len(arrays),
        scratch_shapes=[pltpu.SemaphoreType.DMA((arrays[0].shape[0] + len(arrays),))],
        compiler_params=pltpu.CompilerParams(vmem_limit_bytes=MIB),
        name="hand_on",
    )(*arrays)


def body(saved_codes, relu_mask, errors, decoders, inputs, n):
    latents = saved_codes.shape[1]
    width = errors.shape[2]
    operands = (saved_codes[0], relu_mask[0], errors[0], decoders.reshape(n * latents, width), inputs[0])
    held = exchange(n, *(pltpu.with_memory_space_constraint(x, pltpu.HBM) for x in operands))
    return tuple(result[None] for result in hand_on(*held))


def solution(mesh):
    return jax.shard_map(
        functools.partial(body, n=mesh.shape["layer"]),
        mesh=mesh,
        in_specs=(
            P("layer", "lat", None),
            P("layer", "lat", None),
            P("layer", None, None),
            P("layer", None, "lat", None),
            P("layer", None, None),
        ),
        out_specs=(P("layer", None, "lat", None), P("layer", "lat", None), P("layer", "lat", None)),
        check_vma=False,
    )
```

```python
import functools

import jax
import jax.numpy as jnp
from jax import lax
from jax.experimental import pallas as pl
from jax.experimental.pallas import tpu as pltpu
from jax.sharding import PartitionSpec as P

MESH = pl.DeviceIdType.MESH
DEPTHS = 2
COLUMNS = 1024
MIB = 1 << 20


def exchange_kernel(
    n, codes_hbm, mask_hbm, errors_hbm, decoders_hbm, inputs_hbm, decoder_grad, code_grad, encoder_grad,
    codes, mask, gathered, errors, slab, terms, twin_terms, outgoing, incoming, stage, pre,
    load_sem, decoder_sem, error_sem, stage_sem,
    gather_send, gather_recv, relay_send, relay_recv,
    twin_send, twin_recv, term_send, term_recv,
):
    me = lax.axis_index("layer")
    core = lax.rem(me, 2)
    chip = me // 2
    twin = me + 1 - 2 * core
    chips = n // 2
    group = chips // 2
    late = chip >= group
    _, latents, tokens = gathered.shape
    width = errors.shape[1]
    decoders = slab.at[pl.ds(0, n * latents)]
    inputs = slab.at[pl.ds(0, tokens)]
    half_rows = 2 * group * latents
    half_tokens = tokens // 2
    depth = width // DEPTHS

    load_codes = pltpu.make_async_copy(codes_hbm, codes, load_sem.at[0])
    load_mask = pltpu.make_async_copy(mask_hbm, mask, load_sem.at[1])
    load_inputs = pltpu.make_async_copy(inputs_hbm, inputs, load_sem.at[2])

    def load_errors(k):
        part = (pl.ds(half_tokens, half_tokens), slice(None))
        if k < DEPTHS:
            part = (pl.ds(0, half_tokens), pl.ds(k * depth, depth))
        return pltpu.make_async_copy(errors_hbm.at[part], errors.at[part], error_sem.at[k])

    def load_decoders(k):
        part = (slice(None), pl.ds(k * depth, depth))
        return pltpu.make_async_copy(decoders_hbm.at[part], decoders.at[part], decoder_sem.at[k])

    load_codes.start()
    load_mask.start()
    for k in range(DEPTHS):
        load_errors(k).start()
        load_decoders(k).start()
    load_errors(DEPTHS).start()
    barrier = pltpu.get_barrier_semaphore()
    pl.semaphore_signal(barrier, inc=1, device_id={"layer": twin}, device_id_type=MESH)
    for other in range(chips):
        @pl.when(other != chip)
        def _():
            pl.semaphore_signal(barrier, inc=1, device_id={"layer": 2 * other + core}, device_id_type=MESH)

    load_codes.wait()
    load_mask.wait()
    gathered[me] = codes[...] * mask[...].astype(jnp.bfloat16)
    pl.semaphore_wait(barrier, chips)

    def send_active(other):
        return pltpu.make_async_remote_copy(
            src_ref=gathered.at[me], dst_ref=gathered.at[me],
            send_sem=gather_send.at[other], recv_sem=gather_recv.at[chip],
            device_id={"layer": 2 * other + core}, device_id_type=MESH,
        )

    def take_active(source):
        place = gathered.at[2 * source + core]
        return pltpu.make_async_remote_copy(
            src_ref=place, dst_ref=place,
            send_sem=gather_send.at[source], recv_sem=gather_recv.at[source],
            device_id={"layer": 2 * source + core}, device_id_type=MESH,
        )

    def relay(source):
        place = gathered.at[2 * source + core]
        return pltpu.make_async_remote_copy(
            src_ref=place, dst_ref=place,
            send_sem=relay_send.at[source], recv_sem=relay_recv.at[source],
            device_id={"layer": twin}, device_id_type=MESH,
        )

    def take_relay(source):
        place = gathered.at[2 * source + 1 - core]
        return pltpu.make_async_remote_copy(
            src_ref=place, dst_ref=place,
            send_sem=relay_send.at[source], recv_sem=relay_recv.at[source],
            device_id={"layer": twin}, device_id_type=MESH,
        )

    for other in reversed(range(chips)):
        @pl.when(other > chip)
        def _():
            send_active(other).start()

    relay(chip).start()

    def send_twin(m):
        return pltpu.make_async_remote_copy(
            src_ref=terms.at[m, 1 - core], dst_ref=twin_terms.at[m],
            send_sem=twin_send.at[m], recv_sem=twin_recv.at[m],
            device_id={"layer": twin}, device_id_type=MESH,
        )

    def send_term(m, place):
        target = (m // 2) * group + place
        return pltpu.make_async_remote_copy(
            src_ref=outgoing.at[m, place], dst_ref=incoming.at[lax.rem(m, 2), chip],
            send_sem=term_send.at[m, place], recv_sem=term_recv.at[lax.rem(m, 2), chip],
            device_id={"layer": 2 * target + core}, device_id_type=MESH,
        )

    def take_term(q, source):
        return pltpu.make_async_remote_copy(
            src_ref=incoming.at[q, source], dst_ref=incoming.at[q, source],
            send_sem=term_send.at[0, 0], recv_sem=term_recv.at[q, source],
            device_id={"layer": 2 * source + core}, device_id_type=MESH,
        )

    def pair_sum(m):
        send_twin(m).wait_recv()
        for place in range(group):
            @pl.when((m // 2) * group + place < chip)
            def _():
                total = terms[m, core, place] + twin_terms[m, place]
                outgoing[m, place] = total.astype(jnp.bfloat16)
                send_term(m, place).start()

    def products(part, columns):
        return lax.dot_general(
            decoders[:, columns], errors[part, columns],
            (((1,), (1,)), ((), ())),
            preferred_element_type=jnp.float32,
        ).reshape(2, group, 2, latents, half_tokens)

    for q in range(2):
        part = pl.ds(q * half_tokens, half_tokens)
        if q == 0:
            for k in range(DEPTHS):
                load_errors(k).wait()
                load_decoders(k).wait()
                product = products(part, pl.ds(k * depth, depth))
                for half in range(2):
                    for parity in range(2):
                        if k == 0:
                            terms[2 * half, parity] = product[half, :, parity]
                        else:
                            terms[2 * half, parity] += product[half, :, parity]
        else:
            load_errors(DEPTHS).wait()
            product = products(part, slice(None))
            for half in range(2):
                for parity in range(2):
                    terms[2 * half + 1, parity] = product[half, :, parity]
        send_twin(q).start()

        @pl.when(late)
        def _():
            send_twin(2 + q).start()

    pair_sum(0)

    @pl.when(late)
    def _():
        pair_sum(2)

    for source in range(chips):
        @pl.when(source == chip - 1)
        def _():
            take_active(source).wait_recv()
            relay(source).start()

    load_inputs.start()

    blocks = width // COLUMNS

    def put(first, i, slot):
        columns = pl.ds(pl.multiple_of(i * COLUMNS, COLUMNS), COLUMNS)
        return pltpu.make_async_copy(
            stage.at[slot], decoder_grad.at[pl.ds(first, 2 * group), :, columns], stage_sem.at[slot]
        )

    def relay_far():
        for source in range(group):
            @pl.when(source < chip - 1)
            def _():
                take_active(source).wait_recv()
                relay(source).start()

    def decoder_rows(first, near):
        @pl.loop(0, blocks)
        def _(i):
            slot = lax.rem(i, 2)

            @pl.when(i >= 2)
            def _():
                put(first, i - 2, slot).wait()

            columns = pl.ds(pl.multiple_of(i * COLUMNS, COLUMNS), COLUMNS)
            products = jnp.dot(
                gathered[first:first + 2 * group].reshape(half_rows, tokens), errors[:, columns],
                preferred_element_type=jnp.float32,
            ).reshape(2 * group, latents, COLUMNS)
            for s in range(2 * group):
                stage[slot, s] = jnp.where(first + s <= me, products[s], 0.0).astype(jnp.bfloat16)
            put(first, i, slot).start()
            if near:
                @pl.when(i == 0)
                def _():
                    pair_sum(1)
                    pair_sum(3)

                @pl.when(i == blocks - 3)
                def _():
                    relay_far()

        put(first, blocks - 2, (blocks - 2) % 2).wait()
        put(first, blocks - 1, (blocks - 1) % 2).wait()

    @pl.when(jnp.logical_not(late))
    def _():
        pair_sum(1)
        stage[0] = jnp.zeros(stage.shape[1:], stage.dtype)
        for i in range(blocks):
            put(2 * group, i, 0).start()

    take_relay(chip).wait_recv()

    @pl.when(late)
    def _():
        for source in range(group, chips):
            @pl.when(source < chip - 1)
            def _():
                take_active(source).wait_recv()
                relay(source).start()

        for source in range(group, chips):
            @pl.when(source < chip)
            def _():
                take_relay(source).wait_recv()
        decoder_rows(2 * group, True)

    @pl.when(jnp.logical_not(late))
    def _():
        relay_far()
        for i in range(blocks):
            put(2 * group, i, 0).wait()

    for source in range(group):
        @pl.when(source < chip)
        def _():
            take_relay(source).wait_recv()
    decoder_rows(0, False)

    half = chip // group
    place = lax.rem(chip, group)
    for q in range(2):
        columns = pl.ds(q * half_tokens, half_tokens)
        own = terms[2 * half + q, core, place]
        code_grad[:, columns] = jnp.where(core == 0, own + twin_terms[2 * half + q, place], own)
        for source in range(chips):
            @pl.when(source > chip)
            def _():
                take_term(q, source).wait_recv()
                code_grad[:, columns] += incoming[q, source].astype(jnp.float32)

    pre[...] = (code_grad[...] * mask[...].astype(jnp.float32)).astype(jnp.bfloat16)
    load_inputs.wait()

    @pl.loop(0, blocks)
    def _(i):
        columns = pl.ds(pl.multiple_of(i * COLUMNS, COLUMNS), COLUMNS)
        encoder_grad[:, columns] = jnp.dot(
            pre[...], inputs[:, columns], preferred_element_type=jnp.float32
        ).astype(jnp.bfloat16)

    relay(chip).wait_send()
    for other in range(chips):
        @pl.when(other < chip)
        def _():
            relay(other).wait_send()
            for q in range(2):
                send_term(2 * (other // group) + q, other % group).wait_send()

        @pl.when(other > chip)
        def _():
            send_active(other).wait_send()

    for m in range(2):
        send_twin(m).wait_send()

    @pl.when(late)
    def _():
        for m in range(2, 4):
            send_twin(m).wait_send()


def exchange(n, codes, mask, errors, decoders, inputs):
    latents, tokens = codes.shape
    width = errors.shape[1]
    chips = n // 2
    group = chips // 2
    half_tokens = tokens // 2
    any_space = pl.BlockSpec(memory_space=pl.ANY)
    dma = pltpu.SemaphoreType.DMA
    return pl.pallas_call(
        functools.partial(exchange_kernel, n),
        out_shape=(
            jax.ShapeDtypeStruct((n, latents, width), jnp.bfloat16),
            jax.ShapeDtypeStruct((latents, tokens), jnp.float32),
            jax.ShapeDtypeStruct((latents, width), jnp.bfloat16),
        ),
        in_specs=[any_space] * 5,
        out_specs=(any_space,) + (pl.BlockSpec(memory_space=pltpu.VMEM),) * 2,
        scratch_shapes=[
            pltpu.VMEM((latents, tokens), jnp.bfloat16),
            pltpu.VMEM((latents, tokens), jnp.int32),
            pltpu.VMEM((n, latents, tokens), jnp.bfloat16),
            pltpu.VMEM((tokens, width), jnp.bfloat16),
            pltpu.VMEM((max(n * latents, tokens), width), jnp.bfloat16),
            pltpu.VMEM((4, 2, group, latents, half_tokens), jnp.float32),
            pltpu.VMEM((4, group, latents, half_tokens), jnp.float32),
            pltpu.VMEM((4, group, latents, half_tokens), jnp.bfloat16),
            pltpu.VMEM((2, chips, latents, half_tokens), jnp.bfloat16),
            pltpu.VMEM((2, 2 * group, latents, COLUMNS), jnp.bfloat16),
            pltpu.VMEM((latents, tokens), jnp.bfloat16),
            dma((3,)), dma((DEPTHS,)), dma((DEPTHS + 1,)), dma((2,)),
            dma((chips,)), dma((chips,)), dma((chips,)), dma((chips,)),
            dma((4,)), dma((4,)), dma((4, group)), dma((2, chips)),
        ],
        compiler_params=pltpu.CompilerParams(
            collective_id=0, has_side_effects=True, vmem_limit_bytes=40 * MIB
        ),
        cost_estimate=pl.CostEstimate(
            flops=(4 * n + 2) * latents * tokens * width,
            bytes_accessed=2 * (2 * n * latents + tokens) * width,
            transcendentals=0,
        ),
        name="exchange",
    )(codes, mask, errors, decoders, inputs)


def hand_on_kernel(*refs):
    count = (len(refs) - 1) // 2
    sems = refs[-1]
    pieces = []
    for source, target in zip(refs[:count], refs[count:-1]):
        if len(source.shape) == 3:
            pieces += [(source.at[i], target.at[i]) for i in range(source.shape[0])]
        else:
            pieces.append((source, target))
    copies = [pltpu.make_async_copy(*piece, sems.at[i]) for i, piece in enumerate(pieces)]
    for copy in copies:
        copy.start()
    for copy in copies:
        copy.wait()


def hand_on(*arrays):
    any_space = pl.BlockSpec(memory_space=pl.ANY)
    return pl.pallas_call(
        hand_on_kernel,
        out_shape=tuple(jax.ShapeDtypeStruct(a.shape, a.dtype) for a in arrays),
        in_specs=[any_space] * len(arrays),
        out_specs=(any_space,) * len(arrays),
        scratch_shapes=[pltpu.SemaphoreType.DMA((arrays[0].shape[0] + len(arrays),))],
        compiler_params=pltpu.CompilerParams(vmem_limit_bytes=MIB),
        name="hand_on",
    )(*arrays)


def body(saved_codes, relu_mask, errors, decoders, inputs, n):
    latents = saved_codes.shape[1]
    width = errors.shape[2]
    operands = (saved_codes[0], relu_mask[0], errors[0], decoders.reshape(n * latents, width), inputs[0])
    held = exchange(n, *(pltpu.with_memory_space_constraint(x, pltpu.HBM) for x in operands))
    return tuple(result[None] for result in hand_on(*held))


def solution(mesh):
    return jax.shard_map(
        functools.partial(body, n=mesh.shape["layer"]),
        mesh=mesh,
        in_specs=(
            P("layer", "lat", None),
            P("layer", "lat", None),
            P("layer", None, None),
            P("layer", None, "lat", None),
            P("layer", None, None),
        ),
        out_specs=(P("layer", None, "lat", None), P("layer", "lat", None), P("layer", "lat", None)),
        check_vma=False,
    )
```
